32 devices in a mesh: fsdp: 8 (over z, x), ctx: 2 (over y), tp: 2 (over core).
Axes of the slice: x: 2, y: 2, z: 4, core: 2. Of those that a mesh axis runs over, the one named last changes fastest.
Arguments:
- tokens: bfloat16 [8, 2048, 768], P('fsdp', ('ctx', 'tp')), may hold values from -6 to 6
- segment_order: int32 [8, 4], P('fsdp'), may hold values from 0 to 3, each once within a row
- ln1_gain: bfloat16 [768], P('fsdp'), may hold values from 0.25 to 1.75
- ln1_bias: bfloat16 [768], P('fsdp'), may hold values from -1.75 to 1.75
- qkv_weight: bfloat16 [3, 768, 768], P(None, 'fsdp', 'tp'), may hold values from -0.21875 to 0.21875
- qv_bias: bfloat16 [2, 12, 64], P(None, 'tp', 'fsdp'), may hold values from -1.75 to 1.75
- out_weight: bfloat16 [768, 768], P('tp', 'fsdp'), may hold values from -3.5 to 3.5
- out_bias: bfloat16 [768], P('fsdp'), may hold values from -1.75 to 1.75
- ln2_gain: bfloat16 [768], P('fsdp'), may hold values from 0.25 to 1.75
- ln2_bias: bfloat16 [768], P('fsdp'), may hold values from -1.75 to 1.75
- up_weight: bfloat16 [768, 3072], P('fsdp', 'tp'), may hold values from -0.21875 to 0.21875
- up_bias: bfloat16 [48, 64], P('tp', 'fsdp'), may hold values from -1.75 to 1.75
- down_weight: bfloat16 [3072, 768], P('tp', 'fsdp'), may hold values from -0.109375 to 0.109375
- down_bias: bfloat16 [768], P('fsdp'), may hold values from -1.75 to 1.75
- cotangent: bfloat16 [8, 2048, 768], P('fsdp', ('ctx', 'tp')), may hold values from -6 to 6
Outputs:
- output: bfloat16 [8, 2048, 768], P('fsdp', ('ctx', 'tp'))
- tokens_grad: bfloat16 [8, 2048, 768], P('fsdp', ('ctx', 'tp'))
- ln1_gain_grad: float32 [768], P('fsdp')
- ln1_bias_grad: float32 [768], P('fsdp')
- qkv_weight_grad: float32 [3, 768, 768], P(None, 'fsdp', 'tp')
- qv_bias_grad: float32 [2, 12, 64], P(None, 'tp', 'fsdp')
- out_weight_grad: float32 [768, 768], P('tp', 'fsdp')
- out_bias_grad: float32 [768], P('fsdp')
- ln2_gain_grad: float32 [768], P('fsdp')
- ln2_bias_grad: float32 [768], P('fsdp')
- up_weight_grad: float32 [768, 3072], P('fsdp', 'tp')
- up_bias_grad: float32 [48, 64], P('tp', 'fsdp')
- down_weight_grad: float32 [3072, 768], P('tp', 'fsdp')
- down_bias_grad: float32 [768], P('fsdp')
The draws below stay inside these ranges and needn't reach their ends.
Inputs may be any that keep to these rules, and one draw needn't show every extreme that they name: Each row is a permutation; stored segment c of sequence s (rows c * 512 onward) holds the tokens at places segment_order[s, c] * 512 onward.
All inputs are finite; a program needn't handle non-finite values.
Results may differ from the reference program's by a relative error of at most 0.02.
Values may be sent and summed in bfloat16 or wider, within the bound.
A program may use at most 192 MiB of HBM per device.

```python
import jax
import jax.numpy as jnp
from jax import lax

D = 768
H = 12
HD = 64
FF = 3072
LEN = 2048
HH = 768
NCH = 4
SEQS = 8


def shard_levels(key, extent, split, smallest, high):
    level, own = 1.0, jax.random.fold_in(key, 6)
    for position, blocks in split:
        steps = jnp.exp(jax.random.uniform(jax.random.fold_in(own, position), (blocks,), jnp.float32, smallest / len(split), high / len(split)))
        level = level * jnp.repeat(steps, extent[position] // blocks).reshape([-1 if axis == position else 1 for axis in range(len(extent))])
    return level


def bell_draw(own_key, dims, scale, most, split=(), held_as=jnp.bfloat16):
    values = scale * jax.random.normal(own_key, dims, jnp.float32)
    if split:
        values = values * shard_levels(own_key, dims, split, -0.22, 0.18)
    return jnp.clip(values, -most, most).astype(held_as)


def setup_inputs(seed: int = 0) -> dict:
    seeds = jax.random.split(jax.random.key(seed), 16)
    return {
        "tokens": bell_draw(seeds[0], (SEQS, LEN, D), 1.0, 6.0, ((0, 8), (1, 4))),
        "segment_order": jax.vmap(lambda own: jax.random.permutation(own, NCH))(jax.random.split(seeds[1], SEQS)).reshape((SEQS, NCH)).astype(jnp.int32),
        "ln1_gain": jnp.clip(1.0 + 0.15 * jax.random.normal(seeds[2], (D,), jnp.float32), 0.25, 1.75).astype(jnp.bfloat16),
        "ln1_bias": bell_draw(seeds[3], (D,), 0.3, 1.75, ((0, 8),)),
        "qkv_weight": bell_draw(seeds[4], (3, D, HH), D ** -0.5, 0.21875, ((1, 8), (2, 2))),
        "qv_bias": bell_draw(seeds[5], (2, H, HD), 0.3, 1.75, ((1, 2), (2, 8))),
        "out_weight": bell_draw(seeds[6], (HH, D), (max(1, HH * 8 // LEN)) ** -0.5, 3.5, ((0, 2), (1, 8))),
        "out_bias": bell_draw(seeds[7], (D,), 0.3, 1.75, ((0, 8),)),
        "ln2_gain": jnp.clip(1.0 + 0.15 * jax.random.normal(seeds[8], (D,), jnp.float32), 0.25, 1.75).astype(jnp.bfloat16),
        "ln2_bias": bell_draw(seeds[9], (D,), 0.3, 1.75, ((0, 8),)),
        "up_weight": bell_draw(seeds[10], (D, FF), D ** -0.5, 0.21875, ((0, 8), (1, 2))),
        "up_bias": bell_draw(seeds[11], (FF // 64, 64), 0.3, 1.75, ((0, 2), (1, 8))),
        "down_weight": bell_draw(seeds[12], (FF, D), FF ** -0.5, 0.109375, ((0, 2), (1, 8))),
        "down_bias": bell_draw(seeds[13], (D,), 0.3, 1.75, ((0, 8),)),
        "cotangent": bell_draw(seeds[14], (SEQS, LEN, D), 1.0, 6.0, ((0, 8), (1, 4))),
    }


EPSILON = 1e-05
MASKED = -1e+30
PRECISE = lax.Precision.HIGHEST

@jax.custom_vjp
def low(v):
    return lax.optimization_barrier(v.astype(jnp.bfloat16)).astype(jnp.float32)

@jax.custom_vjp
def low_back(v):
    return v

def low_keep(v):
    return (low(v), None)

def low_pass(kept, grad):
    return (grad,)

def back_keep(v):
    return (v, None)

def back_low(kept, grad):
    return (low(grad),)
low.defvjp(low_keep, low_pass)
low_back.defvjp(back_keep, back_low)

def norm_rows(values, gain, shift):
    average = lax.optimization_barrier(jnp.mean(values, axis=-1, keepdims=True))
    centred = values - average
    spread = lax.optimization_barrier(jnp.mean(centred * centred, axis=-1, keepdims=True))
    return centred * lax.rsqrt(spread + EPSILON) * gain + shift

def positions(segment_order):
    seq_count, segment_count = segment_order.shape
    segment_size = LEN // segment_count
    spread_order = jnp.broadcast_to(segment_order[:, :, None], (seq_count, segment_count, segment_size)).reshape(seq_count, LEN)
    inside = jnp.arange(LEN, dtype=jnp.int32) % segment_size
    return spread_order * segment_size + inside[None, :]

def attend_block(queries, key_rows, value_rows, query_places, key_places):
    scores = low_back(jnp.einsum('gqhd,gkhd->ghqk', queries, key_rows, precision=PRECISE) * HD ** (-0.5))
    allowed = key_places[:, None, None, :] <= query_places[:, None, :, None]
    scores = jnp.where(allowed, scores, MASKED)
    row_peak = lax.optimization_barrier(jnp.max(scores, axis=-1, keepdims=True))
    shifted = jnp.exp(scores - row_peak)
    weights = shifted / lax.optimization_barrier(jnp.sum(shifted, axis=-1, keepdims=True))
    return jnp.einsum('ghqk,gkhd->gqhd', low(weights), value_rows, precision=PRECISE)

def attention(queries, key_rows, value_rows, places):
    seq_group = queries.shape[0]
    block_rows = min(512, LEN)
    block_count = LEN // block_rows
    query_blocks = jnp.swapaxes(queries.reshape(seq_group, block_count, block_rows, H, HD), 0, 1)
    place_blocks = jnp.swapaxes(places.reshape(seq_group, block_count, block_rows), 0, 1)

    def block_step(bundle):
        return attend_block(bundle[0], key_rows, value_rows, bundle[1], places)
    mixed_heads = lax.map(jax.checkpoint(block_step), (query_blocks, place_blocks))
    return jnp.swapaxes(mixed_heads, 0, 1).reshape(seq_group, LEN, H * HD)

def decoder_layer(tokens, weights, places):
    ln1_gain, ln1_bias, qkv_weight, qv_bias, out_weight, out_bias, ln2_gain, ln2_bias, up_weight, up_bias, down_weight, down_bias = weights
    seq_group = tokens.shape[0]
    normed_one = low(norm_rows(tokens, ln1_gain, ln1_bias)).reshape(-1, D)
    queries = low(low_back(jnp.dot(normed_one, qkv_weight[0], precision=PRECISE) + qv_bias[0].reshape(-1)))
    key_rows = low(low_back(jnp.dot(normed_one, qkv_weight[1], precision=PRECISE)))
    value_rows = low(low_back(jnp.dot(normed_one, qkv_weight[2], precision=PRECISE) + qv_bias[1].reshape(-1)))
    head_shape = (seq_group, LEN, H, HD)
    mixed_heads = attention(queries.reshape(head_shape), key_rows.reshape(head_shape), value_rows.reshape(head_shape), places)
    mixed_heads = low(low_back(mixed_heads)).reshape(-1, H * HD)
    resid_mid = tokens.reshape(-1, D) + low_back(jnp.dot(mixed_heads, out_weight, precision=PRECISE)) + out_bias
    normed_two = low(norm_rows(resid_mid, ln2_gain, ln2_bias))
    pre_act = low_back(jnp.dot(normed_two, up_weight, precision=PRECISE) + up_bias.reshape(-1))
    activated = low(jax.nn.gelu(pre_act, approximate=True))
    result = resid_mid + low_back(jnp.dot(activated, down_weight, precision=PRECISE)) + down_bias
    return result.reshape(seq_group, LEN, D)

def reference(tokens, segment_order, ln1_gain, ln1_bias, qkv_weight, qv_bias, out_weight, out_bias, ln2_gain, ln2_bias, up_weight, up_bias, down_weight, down_bias, cotangent):
    weights = tuple((weight_entry.astype(jnp.float32) for weight_entry in (ln1_gain, ln1_bias, qkv_weight, qv_bias, out_weight, out_bias, ln2_gain, ln2_bias, up_weight, up_bias, down_weight, down_bias)))
    places = positions(segment_order)
    seq_group = 1
    for candidate in range(1, SEQS + 1):
        if SEQS % candidate == 0 and candidate * LEN <= 4096:
            seq_group = candidate
    group_count = SEQS // seq_group

    def group_step(totals, bundle):
        inputs, upstream, group_places = bundle

        def forward(values, params):
            return decoder_layer(values, params, group_places)
        result, pullback = jax.vjp(forward, inputs.astype(jnp.float32), weights)
        input_grad, weight_grads = pullback(upstream.astype(jnp.float32))
        totals = jax.tree.map(jnp.add, totals, weight_grads)
        return (totals, (result.astype(jnp.bfloat16), input_grad.astype(jnp.bfloat16)))
    zero_grads = jax.tree.map(jnp.zeros_like, weights)
    totals, (result, tokens_grad) = lax.scan(group_step, zero_grads, (tokens.reshape(group_count, seq_group, LEN, D), cotangent.reshape(group_count, seq_group, LEN, D), places.reshape(group_count, seq_group, LEN)))
    return (result.reshape(SEQS, LEN, D), tokens_grad.reshape(SEQS, LEN, D), totals[0], totals[1], totals[2], totals[3], totals[4], totals[5], totals[6], totals[7], totals[8], totals[9], totals[10], totals[11])
```

```python
from functools import partial

import jax
import jax.numpy as jnp
from jax import lax
from jax.experimental import pallas as pl
from jax.experimental.pallas import tpu as pltpu
from jax.sharding import PartitionSpec as P

EPSILON = 1e-05
MASKED = -1e30
F32 = jnp.float32
BF16 = jnp.bfloat16
HEAD = 64
PAIR = 2 * HEAD


def norm_rows(values, gain, shift):
    average = jnp.mean(values, axis=-1, keepdims=True)
    centred = values - average
    spread = jnp.mean(centred * centred, axis=-1, keepdims=True)
    return centred * lax.rsqrt(spread + EPSILON) * gain + shift


def norm_back(values, gain, upstream):
    average = jnp.mean(values, axis=-1, keepdims=True)
    centred = values - average
    spread = jnp.mean(centred * centred, axis=-1, keepdims=True)
    inverse = lax.rsqrt(spread + EPSILON)
    unit = centred * inverse
    scaled = upstream * gain
    inner = jnp.mean(scaled * unit, axis=-1, keepdims=True)
    grad = (scaled - jnp.mean(scaled, axis=-1, keepdims=True) - unit * inner) * inverse
    return grad, jnp.sum(upstream * unit, axis=(0, 1)), jnp.sum(upstream, axis=(0, 1))


def swap(values, axis):
    return lax.ppermute(values, axis, [(0, 1), (1, 0)])


def dot(left, right, dims):
    return lax.dot_general(left, right, (dims, ((), ())), preferred_element_type=F32)


def head_parts(matrix):
    lane = lax.broadcasted_iota(jnp.int32, matrix.shape, 1)
    zero = jnp.zeros_like(matrix)
    return jnp.where(lane < HEAD, matrix, zero), jnp.where(lane < HEAD, zero, matrix)


def forward_kernel(
    chunk_count, q_segs, k_segs, q_ref, k_ref, v_ref, o_ref, lse_ref, peak, total, acc
):
    block = q_ref.shape[1]
    seq, qblk = pl.program_id(0), pl.program_id(2)
    q_seg = q_segs[seq, qblk]
    peak[...] = jnp.full(peak.shape, MASKED, F32)
    total[...] = jnp.zeros(total.shape, F32)
    acc[...] = jnp.zeros(acc.shape, F32)
    q_parts = head_parts(q_ref[0] * jnp.asarray(HEAD**-0.5, BF16))

    def chunk(index, diagonal):
        rows = pl.ds(index * block, block)
        keys = k_ref[0, rows, :]
        v_parts = head_parts(v_ref[0, rows, :])
        scales, terms = [], []
        for head in range(2):
            scores = dot(q_parts[head], keys, ((1,), (1,)))
            if diagonal:
                q_at = lax.broadcasted_iota(jnp.int32, scores.shape, 0)
                k_at = lax.broadcasted_iota(jnp.int32, scores.shape, 1)
                scores = jnp.where(k_at <= q_at, scores, MASKED)
            old = peak[head]
            new = jnp.maximum(old, jnp.max(scores, axis=1, keepdims=True))
            probs = jnp.exp(scores - new[:, :1])
            scale = jnp.exp(old - new)
            total[head] = total[head] * scale + jnp.sum(probs, axis=1, keepdims=True)
            peak[head] = new
            scales.append(scale)
            terms.append(dot(probs.astype(BF16), v_parts[head], ((1,), (0,))))
        lane = lax.broadcasted_iota(jnp.int32, acc.shape, 1)
        acc[...] = acc[...] * jnp.where(lane < HEAD, scales[0], scales[1]) + (terms[0] + terms[1])

    for index in range(chunk_count):
        k_seg = k_segs[seq, index]
        pl.when(k_seg == q_seg)(partial(chunk, index, True))
        pl.when(k_seg < q_seg)(partial(chunk, index, False))
    lane = lax.broadcasted_iota(jnp.int32, acc.shape, 1)
    sums = jnp.where(lane < HEAD, total[0], total[1])
    o_ref[0] = (acc[...] / sums).astype(BF16)
    lse = jnp.transpose(jnp.where(lane < HEAD, peak[0], peak[1]) + jnp.log(sums))
    lse_ref[0, 0] = jnp.concatenate([lse[0:4], lse[HEAD : HEAD + 4]], axis=0)


def backward_kernel(
    chunk_count,
    q_segs,
    k_segs,
    q_ref,
    g_ref,
    o_ref,
    lse_ref,
    k_ref,
    v_ref,
    dq_ref,
    dkv_ref,
    dq_acc,
    dk_acc,
    dv_acc,
):
    block = q_ref.shape[1]
    seq, qblk = pl.program_id(0), pl.program_id(2)
    q_seg = q_segs[seq, qblk]

    @pl.when(qblk == 0)
    def _():
        dk_acc[...] = jnp.zeros(dk_acc.shape, F32)
        dv_acc[...] = jnp.zeros(dv_acc.shape, F32)

    dq_acc[...] = jnp.zeros(dq_acc.shape, F32)
    q_parts = head_parts(q_ref[0] * jnp.asarray(HEAD**-0.5, BF16))
    g_parts = head_parts(g_ref[0])
    products = jnp.transpose(g_ref[0].astype(F32) * o_ref[0].astype(F32))
    deltas = (
        jnp.sum(products[:HEAD], axis=0, keepdims=True),
        jnp.sum(products[HEAD:], axis=0, keepdims=True),
    )
    lses = (lse_ref[0, 0, 0:1, :], lse_ref[0, 0, 4:5, :])

    def chunk(index, diagonal):
        rows = pl.ds(index * block, block)
        keys = k_ref[0, rows, :]
        values = v_ref[0, rows, :]
        k_parts = head_parts(keys)
        dk, dv, dq = dk_acc[rows, :], dv_acc[rows, :], dq_acc[...]
        for head in range(2):
            scores = dot(keys, q_parts[head], ((1,), (1,)))
            if diagonal:
                k_at = lax.broadcasted_iota(jnp.int32, scores.shape, 0)
                q_at = lax.broadcasted_iota(jnp.int32, scores.shape, 1)
                scores = jnp.where(k_at <= q_at, scores, MASKED)
            probs = jnp.exp(scores - lses[head])
            up = dot(values, g_parts[head], ((1,), (1,)))
            scaled = (probs * (up - deltas[head])).astype(BF16)
            dv = dv + dot(probs.astype(BF16), g_parts[head], ((1,), (0,)))
            dk = dk + dot(scaled, q_parts[head], ((1,), (0,)))
            dq = dq + dot(scaled, k_parts[head], ((0,), (0,)))
        dk_acc[rows, :] = dk
        dv_acc[rows, :] = dv
        dq_acc[...] = dq

    for index in range(chunk_count):
        k_seg = k_segs[seq, index]
        pl.when(k_seg == q_seg)(partial(chunk, index, True))
        pl.when(k_seg < q_seg)(partial(chunk, index, False))
    dq_ref[0] = (dq_acc[...] * HEAD**-0.5).astype(BF16)

    @pl.when(qblk == pl.num_programs(2) - 1)
    def _():
        dkv_ref[0, 0] = dk_acc[...].astype(BF16)
        dkv_ref[0, 1] = dv_acc[...].astype(BF16)


def attend(queries, kv_all, q_segs, k_segs, block):
    seqs, rows, width = queries.shape
    total_len = kv_all.shape[1]
    pairs = width // PAIR
    q_spec = pl.BlockSpec((1, block, PAIR), lambda s, p, q, *_: (s, q, p))
    return pl.pallas_call(
        partial(forward_kernel, total_len // block),
        grid_spec=pltpu.PrefetchScalarGridSpec(
            num_scalar_prefetch=2,
            grid=(seqs, pairs, rows // block),
            in_specs=[
                q_spec,
                pl.BlockSpec((1, total_len, PAIR), lambda s, p, q, *_: (s, 0, p)),
                pl.BlockSpec((1, total_len, PAIR), lambda s, p, q, *_: (s, 0, p + pairs)),
            ],
            out_specs=[
                q_spec,
                pl.BlockSpec((1, 1, 8, block), lambda s, p, q, *_: (s, p, 0, q)),
            ],
            scratch_shapes=[
                pltpu.VMEM((2, block, PAIR), F32),
                pltpu.VMEM((2, block, PAIR), F32),
                pltpu.VMEM((block, PAIR), F32),
            ],
        ),
        out_shape=[
            jax.ShapeDtypeStruct(queries.shape, BF16),
            jax.ShapeDtypeStruct((seqs, pairs, 8, rows), F32),
        ],
        compiler_params=pltpu.CompilerParams(vmem_limit_bytes=40 * 2**20),
        cost_estimate=pl.CostEstimate(
            flops=16 * seqs * rows * total_len * width,
            bytes_accessed=8 * seqs * total_len * width,
            transcendentals=seqs * rows * total_len * width // HEAD,
        ),
    )(q_segs, k_segs, queries, kv_all, kv_all)


def attend_back(queries, grads, mixed, lse, kv_all, q_segs, k_segs, block):
    seqs, rows, width = queries.shape
    total_len = kv_all.shape[1]
    pairs = width // PAIR
    q_spec = pl.BlockSpec((1, block, PAIR), lambda s, p, q, *_: (s, q, p))
    return pl.pallas_call(
        partial(backward_kernel, total_len // block),
        grid_spec=pltpu.PrefetchScalarGridSpec(
            num_scalar_prefetch=2,
            grid=(seqs, pairs, rows // block),
            in_specs=[
                q_spec,
                q_spec,
                q_spec,
                pl.BlockSpec((1, 1, 8, block), lambda s, p, q, *_: (s, p, 0, q)),
                pl.BlockSpec((1, total_len, PAIR), lambda s, p, q, *_: (s, 0, p)),
                pl.BlockSpec((1, total_len, PAIR), lambda s, p, q, *_: (s, 0, p + pairs)),
            ],
            out_specs=[
                q_spec,
                pl.BlockSpec((1, 2, total_len, PAIR), lambda s, p, q, *_: (s, 0, 0, p)),
            ],
            scratch_shapes=[
                pltpu.VMEM((block, PAIR), F32),
                pltpu.VMEM((total_len, PAIR), F32),
                pltpu.VMEM((total_len, PAIR), F32),
            ],
        ),
        out_shape=[
            jax.ShapeDtypeStruct(queries.shape, BF16),
            jax.ShapeDtypeStruct((seqs, 2, total_len, width), BF16),
        ],
        compiler_params=pltpu.CompilerParams(vmem_limit_bytes=48 * 2**20),
        cost_estimate=pl.CostEstimate(
            flops=40 * seqs * rows * total_len * width,
            bytes_accessed=16 * seqs * total_len * width,
            transcendentals=seqs * rows * total_len * width // HEAD,
        ),
    )(q_segs, k_segs, queries, grads, mixed, lse, kv_all, kv_all)


def pair_rows(values):
    return jnp.concatenate([values, swap(values, "tp")], axis=1)


def pair_sum(terms, half_rows):
    terms = terms.reshape(-1, 2 * half_rows, terms.shape[-1])
    other = swap(terms[:, half_rows:].astype(BF16), "tp")
    return terms[:, :half_rows].astype(BF16).astype(F32) + other.astype(F32)


def context_total(values):
    if lax.axis_size("ctx") == 2:
        return values.astype(F32) + swap(values, "ctx").astype(F32)
    return lax.psum(values, "ctx").astype(F32)


def local(
    tokens,
    segment_order,
    ln1_gain,
    ln1_bias,
    qkv_weight,
    qv_bias,
    out_weight,
    out_bias,
    ln2_gain,
    ln2_bias,
    up_weight,
    up_bias,
    down_weight,
    down_bias,
    cotangent,
):
    shards = lax.axis_size("fsdp")
    contexts = lax.axis_size("ctx")
    seq_count, half_rows, model_width = tokens.shape
    local_rows = half_rows * 2
    depth = model_width // shards
    inner_width = qkv_weight.shape[2]
    heads = qv_bias.shape[1]
    hidden = up_weight.shape[1]
    units = up_bias.shape[0]
    qkv_width = 3 * inner_width

    smalls = [ln1_gain, ln1_bias, out_bias, ln2_gain, ln2_bias, down_bias]
    flat = jnp.concatenate([part.reshape(-1) for part in smalls + [qv_bias, up_bias]])
    flat = jnp.pad(flat, (0, qkv_width - flat.shape[0])).reshape(1, qkv_width)
    first = jnp.concatenate(
        [jnp.swapaxes(qkv_weight, 0, 1).reshape(depth, qkv_width), flat], axis=0
    )
    first_all = lax.all_gather(first, "fsdp", axis=0, tiled=False)
    qkv_full = first_all[:, :depth].reshape(model_width, qkv_width)
    small_all = first_all[:, depth].astype(F32)
    gain_one, shift_one, outb_full, gain_two, shift_two, downb_full = [
        small_all[:, i * depth : (i + 1) * depth].reshape(model_width) for i in range(6)
    ]
    start = 6 * depth
    span = qv_bias.shape[2]
    qv_size = 2 * heads * span
    qv_full = jnp.moveaxis(
        small_all[:, start : start + qv_size].reshape(shards, 2, heads, span), 0, 2
    ).reshape(2, inner_width)
    start += qv_size
    upb_full = jnp.moveaxis(
        small_all[:, start : start + units * span].reshape(shards, units, span), 0, 1
    ).reshape(hidden)

    residual_in = tokens.astype(F32)
    normed_one = norm_rows(residual_in, gain_one, shift_one).astype(BF16)
    rows_one = pair_rows(normed_one)
    grad_flat = pair_rows(cotangent).reshape(-1, model_width)
    flat_one = rows_one.reshape(-1, model_width)
    kv = jnp.dot(flat_one, qkv_full[:, inner_width:], preferred_element_type=F32)
    kv_bias = jnp.concatenate([jnp.zeros((inner_width,), F32), qv_full[1]])
    kv = (kv + kv_bias).astype(BF16).reshape(seq_count, local_rows, 2 * inner_width)
    queries = jnp.dot(flat_one, qkv_full[:, :inner_width], preferred_element_type=F32)
    queries = (queries + qv_full[0]).astype(BF16).reshape(seq_count, local_rows, inner_width)

    second = jnp.concatenate([out_weight.T, up_weight, down_weight.T], axis=1)
    kv, second = lax.optimization_barrier((kv, second))
    second_all = lax.all_gather(second, "fsdp", axis=0, tiled=True)
    out_t = second_all[:, :inner_width]
    up_full = second_all[:, inner_width : inner_width + hidden]
    down_t = second_all[:, inner_width + hidden :]

    here, core = lax.axis_index("ctx"), lax.axis_index("tp")
    if contexts == 2:
        kv_all = jnp.concatenate([kv, swap(kv, "ctx")], axis=1)
        order = [here, 1 - here]
    else:
        kv_all = lax.all_gather(kv, "ctx", axis=1, tiled=True)
        order = list(range(contexts))
    segment_size = contexts * local_rows // segment_order.shape[1]
    block = min(segment_size, half_rows)
    per_half = half_rows // segment_size

    def half_segments(context):
        picks = []
        for turn in range(2):
            at = (context * 2 + (core + turn) % 2) * per_half
            picks.append(lax.dynamic_slice_in_dim(segment_order, at, per_half, 1))
        return jnp.concatenate(picks, axis=1)

    q_segs = half_segments(here)
    k_segs = jnp.concatenate([half_segments(context) for context in order], axis=1)
    mixed, lse = attend(queries, kv_all, q_segs, k_segs, block)
    mixed_flat = mixed.reshape(-1, inner_width)

    attn_part = pair_sum(dot(mixed_flat, out_t, ((1,), (1,))), half_rows)
    resid_mid = residual_in + attn_part + outb_full
    normed_two = norm_rows(resid_mid, gain_two, shift_two).astype(BF16)
    flat_two = pair_rows(normed_two).reshape(-1, model_width)
    pre_act = jnp.dot(flat_two, up_full, preferred_element_type=F32) + upb_full
    activated, gelu_pull = jax.vjp(partial(jax.nn.gelu, approximate=True), pre_act)
    activated = activated.astype(BF16)
    act_grad = jnp.dot(grad_flat, down_t, preferred_element_type=F32)
    pre_grad = gelu_pull(act_grad)[0].astype(BF16)
    norm_two_grad = pair_sum(dot(pre_grad, up_full, ((1,), (1,))), half_rows)
    upstream = cotangent.astype(F32)
    mid_grad, gain_two_grad, shift_two_grad = norm_back(resid_mid, gain_two, norm_two_grad)
    resid_grad = upstream + mid_grad
    branch_flat = pair_rows(resid_grad.astype(BF16)).reshape(-1, model_width)
    mixed_grad = jnp.dot(branch_flat, out_t, preferred_element_type=F32).astype(BF16)
    up_grad = dot(flat_two, pre_grad, ((0,), (0,))).astype(BF16)
    down_grad = dot(grad_flat, activated, ((0,), (0,))).astype(BF16)
    out_grad = dot(branch_flat, mixed_flat, ((0,), (0,))).astype(BF16)
    early = jnp.concatenate([out_grad, up_grad, down_grad], axis=1)
    early, mixed_grad = lax.optimization_barrier((early, mixed_grad))
    early_part = lax.psum_scatter(early, "fsdp", scatter_dimension=0, tiled=True)

    query_grad, kv_grad = attend_back(
        queries,
        mixed_grad.reshape(queries.shape),
        mixed,
        lse,
        kv_all,
        q_segs,
        k_segs,
        block,
    )
    if contexts == 2:
        kv_own = kv_grad[:, :, :local_rows].astype(F32)
        kv_own = kv_own + swap(kv_grad[:, :, local_rows:], "ctx").astype(F32)
        kv_own = kv_own.astype(BF16)
    else:
        kv_own = lax.psum_scatter(kv_grad, "ctx", scatter_dimension=2, tiled=True)
    stacked = jnp.concatenate([query_grad, kv_own[:, 0], kv_own[:, 1]], axis=2)
    stacked = stacked.reshape(-1, qkv_width)
    norm_one_grad = pair_sum(dot(stacked, qkv_full, ((1,), (1,))), half_rows)
    qkv_grad = dot(flat_one, stacked, ((0,), (0,)))

    mlp_terms = dot(activated, down_t, ((1,), (1,)))
    mlp_part = pair_sum(mlp_terms, half_rows)
    output = (resid_mid + mlp_part + downb_full).astype(BF16)

    input_part, gain_one_grad, shift_one_grad = norm_back(residual_in, gain_one, norm_one_grad)
    tokens_grad = (resid_grad + input_part).astype(BF16)
    norm_grads = jnp.stack(
        [
            gain_one_grad,
            shift_one_grad,
            jnp.sum(resid_grad, axis=(0, 1)),
            gain_two_grad,
            shift_two_grad,
            jnp.sum(upstream, axis=(0, 1)),
        ]
    )
    norm_grads = norm_grads + swap(norm_grads, "tp")
    bias_sums = jnp.sum(stacked.astype(F32), axis=0)
    qv_grad = jnp.stack([bias_sums[:inner_width], bias_sums[2 * inner_width :]])
    upb_grad = jnp.sum(pre_grad.astype(F32), axis=0)
    small_rows = jnp.concatenate(
        [
            jnp.swapaxes(norm_grads.reshape(6, shards, depth), 0, 1).reshape(shards, -1),
            jnp.moveaxis(qv_grad.reshape(2, heads, shards, span), 2, 0).reshape(shards, -1),
            jnp.moveaxis(upb_grad.reshape(units, shards, span), 1, 0).reshape(shards, -1),
        ],
        axis=1,
    )
    small_rows = jnp.pad(small_rows, ((0, 0), (0, qkv_width - small_rows.shape[1])))
    late = jnp.concatenate(
        [qkv_grad.reshape(shards, depth, qkv_width), small_rows[:, None, :]], axis=1
    ).astype(BF16)
    late_part = lax.psum_scatter(late, "fsdp", scatter_dimension=0, tiled=False)
    early_total = context_total(early_part)
    late_total = context_total(late_part)
    small = late_total[depth]
    start = 6 * depth
    return (
        output,
        tokens_grad,
        small[:depth],
        small[depth : 2 * depth],
        jnp.swapaxes(late_total[:depth].reshape(depth, 3, inner_width), 0, 1),
        small[start : start + qv_size].reshape(2, heads, span),
        early_total[:, :inner_width].T,
        small[2 * depth : 3 * depth],
        small[3 * depth : 4 * depth],
        small[4 * depth : 5 * depth],
        early_total[:, inner_width : inner_width + hidden],
        small[start + qv_size : start + qv_size + units * span].reshape(units, span),
        early_total[:, inner_width + hidden :].T,
        small[5 * depth : 6 * depth],
    )


def solution(mesh):
    placed = (
        P("fsdp", ("ctx", "tp"), None),
        P("fsdp", None),
        P("fsdp"),
        P("fsdp"),
        P(None, "fsdp", "tp"),
        P(None, "tp", "fsdp"),
        P("tp", "fsdp"),
        P("fsdp"),
        P("fsdp"),
        P("fsdp"),
        P("fsdp", "tp"),
        P("tp", "fsdp"),
        P("tp", "fsdp"),
        P("fsdp"),
        P("fsdp", ("ctx", "tp"), None),
    )
    return jax.shard_map(
        local,
        mesh=mesh,
        in_specs=placed,
        out_specs=(
            P("fsdp", ("ctx", "tp"), None),
            P("fsdp", ("ctx", "tp"), None),
            P("fsdp"),
            P("fsdp"),
            P(None, "fsdp", "tp"),
            P(None, "tp", "fsdp"),
            P("tp", "fsdp"),
            P("fsdp"),
            P("fsdp"),
            P("fsdp"),
            P("fsdp", "tp"),
            P("tp", "fsdp"),
            P("tp", "fsdp"),
            P("fsdp"),
        ),
        check_vma=False,
    )
```

```python
from functools import partial

import jax
import jax.numpy as jnp
from jax import lax
from jax.experimental import pallas as pl
from jax.experimental.pallas import tpu as pltpu
from jax.sharding import PartitionSpec as P

EPSILON = 1e-05
MASKED = -1e30
F32 = jnp.float32
BF16 = jnp.bfloat16
HEAD = 64
PAIR = 2 * HEAD


def norm_rows(values, gain, shift):
    average = jnp.mean(values, axis=-1, keepdims=True)
    centred = values - average
    spread = jnp.mean(centred * centred, axis=-1, keepdims=True)
    return centred * lax.rsqrt(spread + EPSILON) * gain + shift


def norm_back(values, gain, upstream):
    average = jnp.mean(values, axis=-1, keepdims=True)
    centred = values - average
    spread = jnp.mean(centred * centred, axis=-1, keepdims=True)
    inverse = lax.rsqrt(spread + EPSILON)
    unit = centred * inverse
    scaled = upstream * gain
    inner = jnp.mean(scaled * unit, axis=-1, keepdims=True)
    grad = (scaled - jnp.mean(scaled, axis=-1, keepdims=True) - unit * inner) * inverse
    return grad, jnp.sum(upstream * unit, axis=(0, 1)), jnp.sum(upstream, axis=(0, 1))


def swap(values, axis):
    return lax.ppermute(values, axis, [(0, 1), (1, 0)])


def dot(left, right, dims):
    return lax.dot_general(left, right, (dims, ((), ())), preferred_element_type=F32)


def head_parts(matrix):
    lane = lax.broadcasted_iota(jnp.int32, matrix.shape, 1)
    zero = jnp.zeros_like(matrix)
    return jnp.where(lane < HEAD, matrix, zero), jnp.where(lane < HEAD, zero, matrix)


def forward_kernel(
    chunk_count, q_segs, k_segs, q_ref, k_ref, v_ref, o_ref, lse_ref, peak, total, acc
):
    block = q_ref.shape[1]
    seq, qblk = pl.program_id(0), pl.program_id(2)
    q_seg = q_segs[seq, qblk]
    peak[...] = jnp.full(peak.shape, MASKED, F32)
    total[...] = jnp.zeros(total.shape, F32)
    acc[...] = jnp.zeros(acc.shape, F32)
    q_parts = head_parts(q_ref[0] * jnp.asarray(HEAD**-0.5, BF16))

    def chunk(index, diagonal):
        rows = pl.ds(index * block, block)
        keys = k_ref[0, rows, :]
        v_parts = head_parts(v_ref[0, rows, :])
        scales, terms = [], []
        for head in range(2):
            scores = dot(q_parts[head], keys, ((1,), (1,)))
            if diagonal:
                q_at = lax.broadcasted_iota(jnp.int32, scores.shape, 0)
                k_at = lax.broadcasted_iota(jnp.int32, scores.shape, 1)
                scores = jnp.where(k_at <= q_at, scores, MASKED)
            old = peak[head]
            new = jnp.maximum(old, jnp.max(scores, axis=1, keepdims=True))
            probs = jnp.exp(scores - new[:, :1])
            scale = jnp.exp(old - new)
            total[head] = total[head] * scale + jnp.sum(probs, axis=1, keepdims=True)
            peak[head] = new
            scales.append(scale)
            terms.append(dot(probs.astype(BF16), v_parts[head], ((1,), (0,))))
        lane = lax.broadcasted_iota(jnp.int32, acc.shape, 1)
        acc[...] = acc[...] * jnp.where(lane < HEAD, scales[0], scales[1]) + (terms[0] + terms[1])

    for index in range(chunk_count):
        k_seg = k_segs[seq, index]
        pl.when(k_seg == q_seg)(partial(chunk, index, True))
        pl.when(k_seg < q_seg)(partial(chunk, index, False))
    lane = lax.broadcasted_iota(jnp.int32, acc.shape, 1)
    sums = jnp.where(lane < HEAD, total[0], total[1])
    o_ref[0] = (acc[...] / sums).astype(BF16)
    lse = jnp.transpose(jnp.where(lane < HEAD, peak[0], peak[1]) + jnp.log(sums))
    lse_ref[0, 0] = jnp.concatenate([lse[0:4], lse[HEAD : HEAD + 4]], axis=0)


def backward_kernel(
    chunk_count,
    q_segs,
    k_segs,
    q_ref,
    g_ref,
    o_ref,
    lse_ref,
    k_ref,
    v_ref,
    dq_ref,
    dkv_ref,
    dq_acc,
    dk_acc,
    dv_acc,
):
    block = q_ref.shape[1]
    seq, qblk = pl.program_id(0), pl.program_id(2)
    q_seg = q_segs[seq, qblk]

    @pl.when(qblk == 0)
    def _():
        dk_acc[...] = jnp.zeros(dk_acc.shape, F32)
        dv_acc[...] = jnp.zeros(dv_acc.shape, F32)

    dq_acc[...] = jnp.zeros(dq_acc.shape, F32)
    q_parts = head_parts(q_ref[0] * jnp.asarray(HEAD**-0.5, BF16))
    g_parts = head_parts(g_ref[0])
    products = jnp.transpose(g_ref[0].astype(F32) * o_ref[0].astype(F32))
    deltas = (
        jnp.sum(products[:HEAD], axis=0, keepdims=True),
        jnp.sum(products[HEAD:], axis=0, keepdims=True),
    )
    lses = (lse_ref[0, 0, 0:1, :], lse_ref[0, 0, 4:5, :])

    def chunk(index, diagonal):
        rows = pl.ds(index * block, block)
        keys = k_ref[0, rows, :]
        values = v_ref[0, rows, :]
        k_parts = head_parts(keys)
        dk, dv, dq = dk_acc[rows, :], dv_acc[rows, :], dq_acc[...]
        for head in range(2):
            scores = dot(keys, q_parts[head], ((1,), (1,)))
            if diagonal:
                k_at = lax.broadcasted_iota(jnp.int32, scores.shape, 0)
                q_at = lax.broadcasted_iota(jnp.int32, scores.shape, 1)
                scores = jnp.where(k_at <= q_at, scores, MASKED)
            probs = jnp.exp(scores - lses[head])
            up = dot(values, g_parts[head], ((1,), (1,)))
            scaled = (probs * (up - deltas[head])).astype(BF16)
            dv = dv + dot(probs.astype(BF16), g_parts[head], ((1,), (0,)))
            dk = dk + dot(scaled, q_parts[head], ((1,), (0,)))
            dq = dq + dot(scaled, k_parts[head], ((0,), (0,)))
        dk_acc[rows, :] = dk
        dv_acc[rows, :] = dv
        dq_acc[...] = dq

    for index in range(chunk_count):
        k_seg = k_segs[seq, index]
        pl.when(k_seg == q_seg)(partial(chunk, index, True))
        pl.when(k_seg < q_seg)(partial(chunk, index, False))
    dq_ref[0] = (dq_acc[...] * HEAD**-0.5).astype(BF16)

    @pl.when(qblk == pl.num_programs(2) - 1)
    def _():
        dkv_ref[0, 0] = dk_acc[...].astype(BF16)
        dkv_ref[0, 1] = dv_acc[...].astype(BF16)


def attend(queries, kv_all, q_segs, k_segs, block):
    seqs, rows, width = queries.shape
    total_len = kv_all.shape[1]
    pairs = width // PAIR
    q_spec = pl.BlockSpec((1, block, PAIR), lambda s, p, q, *_: (s, q, p))
    return pl.pallas_call(
        partial(forward_kernel, total_len // block),
        grid_spec=pltpu.PrefetchScalarGridSpec(
            num_scalar_prefetch=2,
            grid=(seqs, pairs, rows // block),
            in_specs=[
                q_spec,
                pl.BlockSpec((1, total_len, PAIR), lambda s, p, q, *_: (s, 0, p)),
                pl.BlockSpec((1, total_len, PAIR), lambda s, p, q, *_: (s, 0, p + pairs)),
            ],
            out_specs=[
                q_spec,
                pl.BlockSpec((1, 1, 8, block), lambda s, p, q, *_: (s, p, 0, q)),
            ],
            scratch_shapes=[
                pltpu.VMEM((2, block, PAIR), F32),
                pltpu.VMEM((2, block, PAIR), F32),
                pltpu.VMEM((block, PAIR), F32),
            ],
        ),
        out_shape=[
            jax.ShapeDtypeStruct(queries.shape, BF16),
            jax.ShapeDtypeStruct((seqs, pairs, 8, rows), F32),
        ],
        compiler_params=pltpu.CompilerParams(vmem_limit_bytes=40 * 2**20),
        cost_estimate=pl.CostEstimate(
            flops=16 * seqs * rows * total_len * width,
            bytes_accessed=8 * seqs * total_len * width,
            transcendentals=seqs * rows * total_len * width // HEAD,
        ),
    )(q_segs, k_segs, queries, kv_all, kv_all)


def attend_back(queries, grads, mixed, lse, kv_all, q_segs, k_segs, block):
    seqs, rows, width = queries.shape
    total_len = kv_all.shape[1]
    pairs = width // PAIR
    q_spec = pl.BlockSpec((1, block, PAIR), lambda s, p, q, *_: (s, q, p))
    return pl.pallas_call(
        partial(backward_kernel, total_len // block),
        grid_spec=pltpu.PrefetchScalarGridSpec(
            num_scalar_prefetch=2,
            grid=(seqs, pairs, rows // block),
            in_specs=[
                q_spec,
                q_spec,
                q_spec,
                pl.BlockSpec((1, 1, 8, block), lambda s, p, q, *_: (s, p, 0, q)),
                pl.BlockSpec((1, total_len, PAIR), lambda s, p, q, *_: (s, 0, p)),
                pl.BlockSpec((1, total_len, PAIR), lambda s, p, q, *_: (s, 0, p + pairs)),
            ],
            out_specs=[
                q_spec,
                pl.BlockSpec((1, 2, total_len, PAIR), lambda s, p, q, *_: (s, 0, 0, p)),
            ],
            scratch_shapes=[
                pltpu.VMEM((block, PAIR), F32),
                pltpu.VMEM((total_len, PAIR), F32),
                pltpu.VMEM((total_len, PAIR), F32),
            ],
        ),
        out_shape=[
            jax.ShapeDtypeStruct(queries.shape, BF16),
            jax.ShapeDtypeStruct((seqs, 2, total_len, width), BF16),
        ],
        compiler_params=pltpu.CompilerParams(vmem_limit_bytes=48 * 2**20),
        cost_estimate=pl.CostEstimate(
            flops=40 * seqs * rows * total_len * width,
            bytes_accessed=16 * seqs * total_len * width,
            transcendentals=seqs * rows * total_len * width // HEAD,
        ),
    )(q_segs, k_segs, queries, grads, mixed, lse, kv_all, kv_all)


def pair_rows(values):
    return jnp.concatenate([values, swap(values, "tp")], axis=1)


def pair_sum(terms, half_rows):
    terms = terms.reshape(-1, 2 * half_rows, terms.shape[-1])
    other = swap(terms[:, half_rows:].astype(BF16), "tp")
    return terms[:, :half_rows].astype(BF16).astype(F32) + other.astype(F32)


def axis_bits():
    return (lax.axis_size("fsdp") - 1).bit_length()


def halving_orders():
    bits = axis_bits()
    highest = list(range(bits - 1, 0, -1))
    if lax.axis_size("ctx") == 2:
        return (
            ["ctx", 0] + highest,
            [0] + highest[:1] + ["ctx"] + highest[1:],
        )
    return [0] + highest, highest[:1] + [0] + highest[1:]


def flip(values, bit):
    if bit == "ctx":
        return swap(values, "ctx")
    count = lax.axis_size("fsdp")
    return lax.ppermute(values, "fsdp", [(i, i ^ (1 << bit)) for i in range(count)])


def own_bit(bit):
    if bit == "ctx":
        return lax.axis_index("ctx")
    return (lax.axis_index("fsdp") >> bit) & 1


def scatter_sum(values, order):
    shards, rows, columns = values.shape
    bits = axis_bits()
    left = list(range(bits - 1, -1, -1))
    if "ctx" in order:
        left.append("ctx")
        rows //= 2
    values = values.reshape((2,) * len(left) + (rows, columns))
    for bit in order:
        at, mine = left.index(bit), own_bit(bit)
        sent = lax.dynamic_index_in_dim(values, 1 - mine, at, keepdims=False)
        kept = lax.dynamic_index_in_dim(values, mine, at, keepdims=False)
        values = kept.astype(F32) + flip(sent, bit).astype(F32)
        if len(left) > 1:
            values = values.astype(sent.dtype)
        left.remove(bit)
    if "ctx" not in order:
        if lax.axis_size("ctx") == 2:
            return values + swap(values, "ctx")
        return lax.psum(values.astype(BF16), "ctx").astype(F32)
    values = values.astype(BF16)
    other = swap(values, "ctx")
    first = lax.axis_index("ctx") == 0
    low, high = jnp.where(first, values, other), jnp.where(first, other, values)
    return jnp.concatenate([low, high], axis=0).astype(F32)


def local(
    tokens,
    segment_order,
    ln1_gain,
    ln1_bias,
    qkv_weight,
    qv_bias,
    out_weight,
    out_bias,
    ln2_gain,
    ln2_bias,
    up_weight,
    up_bias,
    down_weight,
    down_bias,
    cotangent,
):
    shards = lax.axis_size("fsdp")
    contexts = lax.axis_size("ctx")
    seq_count, half_rows, model_width = tokens.shape
    local_rows = half_rows * 2
    depth = model_width // shards
    inner_width = qkv_weight.shape[2]
    heads = qv_bias.shape[1]
    hidden = up_weight.shape[1]
    units = up_bias.shape[0]
    qkv_width = 3 * inner_width

    smalls = [ln1_gain, ln1_bias, out_bias, ln2_gain, ln2_bias, down_bias]
    flat = jnp.concatenate([part.reshape(-1) for part in smalls + [qv_bias, up_bias]])
    flat = jnp.pad(flat, (0, qkv_width - flat.shape[0])).reshape(1, qkv_width)
    first = jnp.concatenate(
        [jnp.swapaxes(qkv_weight, 0, 1).reshape(depth, qkv_width), flat], axis=0
    )
    first_all = lax.all_gather(first, "fsdp", axis=0, tiled=False)
    qkv_full = first_all[:, :depth].reshape(model_width, qkv_width)
    small_all = first_all[:, depth].astype(F32)
    gain_one, shift_one, outb_full, gain_two, shift_two, downb_full = [
        small_all[:, i * depth : (i + 1) * depth].reshape(model_width) for i in range(6)
    ]
    start = 6 * depth
    span = qv_bias.shape[2]
    qv_size = 2 * heads * span
    qv_full = jnp.moveaxis(
        small_all[:, start : start + qv_size].reshape(shards, 2, heads, span), 0, 2
    ).reshape(2, inner_width)
    start += qv_size
    upb_full = jnp.moveaxis(
        small_all[:, start : start + units * span].reshape(shards, units, span), 0, 1
    ).reshape(hidden)

    residual_in = tokens.astype(F32)
    normed_one = norm_rows(residual_in, gain_one, shift_one).astype(BF16)
    rows_one = pair_rows(normed_one)
    grad_flat = pair_rows(cotangent).reshape(-1, model_width)
    flat_one = rows_one.reshape(-1, model_width)
    kv = jnp.dot(flat_one, qkv_full[:, inner_width:], preferred_element_type=F32)
    kv_bias = jnp.concatenate([jnp.zeros((inner_width,), F32), qv_full[1]])
    kv = (kv + kv_bias).astype(BF16).reshape(seq_count, local_rows, 2 * inner_width)
    queries = jnp.dot(flat_one, qkv_full[:, :inner_width], preferred_element_type=F32)
    queries = (queries + qv_full[0]).astype(BF16).reshape(seq_count, local_rows, inner_width)

    second = jnp.concatenate([out_weight.T, up_weight, down_weight.T], axis=1)
    kv, second = lax.optimization_barrier((kv, second))
    second_all = lax.all_gather(second, "fsdp", axis=0, tiled=True)
    out_t = second_all[:, :inner_width]
    up_full = second_all[:, inner_width : inner_width + hidden]
    down_t = second_all[:, inner_width + hidden :]

    here, core = lax.axis_index("ctx"), lax.axis_index("tp")
    if contexts == 2:
        kv_all = jnp.concatenate([kv, swap(kv, "ctx")], axis=1)
        order = [here, 1 - here]
    else:
        kv_all = lax.all_gather(kv, "ctx", axis=1, tiled=True)
        order = list(range(contexts))
    segment_size = contexts * local_rows // segment_order.shape[1]
    block = min(segment_size, half_rows)
    per_half = half_rows // segment_size

    def half_segments(context):
        picks = []
        for turn in range(2):
            at = (context * 2 + (core + turn) % 2) * per_half
            picks.append(lax.dynamic_slice_in_dim(segment_order, at, per_half, 1))
        return jnp.concatenate(picks, axis=1)

    q_segs = half_segments(here)
    k_segs = jnp.concatenate([half_segments(context) for context in order], axis=1)
    mixed, lse = attend(queries, kv_all, q_segs, k_segs, block)
    mixed_flat = mixed.reshape(-1, inner_width)

    attn_part = pair_sum(dot(mixed_flat, out_t, ((1,), (1,))), half_rows)
    resid_mid = residual_in + attn_part + outb_full
    normed_two = norm_rows(resid_mid, gain_two, shift_two).astype(BF16)
    flat_two = pair_rows(normed_two).reshape(-1, model_width)
    pre_act = jnp.dot(flat_two, up_full, preferred_element_type=F32) + upb_full
    activated, gelu_pull = jax.vjp(partial(jax.nn.gelu, approximate=True), pre_act)
    activated = activated.astype(BF16)
    act_grad = jnp.dot(grad_flat, down_t, preferred_element_type=F32)
    pre_grad = gelu_pull(act_grad)[0].astype(BF16)
    norm_two_grad = pair_sum(dot(pre_grad, up_full, ((1,), (1,))), half_rows)
    upstream = cotangent.astype(F32)
    mid_grad, gain_two_grad, shift_two_grad = norm_back(resid_mid, gain_two, norm_two_grad)
    resid_grad = upstream + mid_grad
    branch_flat = pair_rows(resid_grad.astype(BF16)).reshape(-1, model_width)
    mixed_grad = jnp.dot(branch_flat, out_t, preferred_element_type=F32).astype(BF16)
    up_grad = dot(flat_two, pre_grad, ((0,), (0,))).astype(BF16)
    down_grad = dot(grad_flat, activated, ((0,), (0,))).astype(BF16)
    out_grad = dot(branch_flat, mixed_flat, ((0,), (0,))).astype(BF16)
    wide = jnp.concatenate([up_grad, out_grad], axis=1)
    wide, down_grad, mixed_grad = lax.optimization_barrier((wide, down_grad, mixed_grad))
    order_a, order_b = halving_orders()
    down_total = scatter_sum(down_grad.reshape(shards, depth, hidden), order_a)
    wide_total = scatter_sum(wide.reshape(shards, depth, hidden + inner_width), order_b)

    query_grad, kv_grad = attend_back(
        queries,
        mixed_grad.reshape(queries.shape),
        mixed,
        lse,
        kv_all,
        q_segs,
        k_segs,
        block,
    )
    if contexts == 2:
        kv_own = kv_grad[:, :, :local_rows].astype(F32)
        kv_own = kv_own + swap(kv_grad[:, :, local_rows:], "ctx").astype(F32)
        kv_own = kv_own.astype(BF16)
    else:
        kv_own = lax.psum_scatter(kv_grad, "ctx", scatter_dimension=2, tiled=True)
    stacked = jnp.concatenate([query_grad, kv_own[:, 0], kv_own[:, 1]], axis=2)
    stacked = stacked.reshape(-1, qkv_width)
    norm_one_grad = pair_sum(dot(stacked, qkv_full, ((1,), (1,))), half_rows)
    qkv_grad = dot(flat_one, stacked, ((0,), (0,))).astype(BF16)
    cut = -(-qkv_width // 256) * 128
    qkv_grad = qkv_grad.reshape(shards, depth, qkv_width)
    qkv_total = jnp.concatenate(
        [
            scatter_sum(qkv_grad[:, :, :cut], order_a),
            scatter_sum(qkv_grad[:, :, cut:], order_b),
        ],
        axis=1,
    )

    mlp_terms = dot(activated, down_t, ((1,), (1,)))
    mlp_part = pair_sum(mlp_terms, half_rows)
    output = (resid_mid + mlp_part + downb_full).astype(BF16)

    input_part, gain_one_grad, shift_one_grad = norm_back(residual_in, gain_one, norm_one_grad)
    tokens_grad = (resid_grad + input_part).astype(BF16)
    norm_grads = jnp.stack(
        [
            gain_one_grad,
            shift_one_grad,
            jnp.sum(resid_grad, axis=(0, 1)),
            gain_two_grad,
            shift_two_grad,
            jnp.sum(upstream, axis=(0, 1)),
        ]
    )
    norm_grads = norm_grads + swap(norm_grads, "tp")
    bias_sums = jnp.sum(stacked.astype(F32), axis=0)
    qv_grad = jnp.stack([bias_sums[:inner_width], bias_sums[2 * inner_width :]])
    upb_grad = jnp.sum(pre_grad.astype(F32), axis=0)
    small_rows = jnp.concatenate(
        [
            jnp.swapaxes(norm_grads.reshape(6, shards, depth), 0, 1).reshape(shards, -1),
            jnp.moveaxis(qv_grad.reshape(2, heads, shards, span), 2, 0).reshape(shards, -1),
            jnp.moveaxis(upb_grad.reshape(units, shards, span), 1, 0).reshape(shards, -1),
        ],
        axis=1,
    )
    small_size = -(-small_rows.shape[1] // 1024) * 1024
    small_rows = jnp.pad(small_rows, ((0, 0), (0, small_size - small_rows.shape[1])))
    small = small_rows.reshape(shards, small_size // 128, 128)
    plain = [bit for bit in order_a if bit != "ctx"]
    small = scatter_sum(small, plain).reshape(small_size)
    start = 6 * depth
    return (
        output,
        tokens_grad,
        small[:depth],
        small[depth : 2 * depth],
        jnp.swapaxes(qkv_total.reshape(depth, 3, inner_width), 0, 1),
        small[start : start + qv_size].reshape(2, heads, span),
        wide_total[:, hidden:].T,
        small[2 * depth : 3 * depth],
        small[3 * depth : 4 * depth],
        small[4 * depth : 5 * depth],
        wide_total[:, :hidden],
        small[start + qv_size : start + qv_size + units * span].reshape(units, span),
        down_total.T,
        small[5 * depth : 6 * depth],
    )


def solution(mesh):
    placed = (
        P("fsdp", ("ctx", "tp"), None),
        P("fsdp", None),
        P("fsdp"),
        P("fsdp"),
        P(None, "fsdp", "tp"),
        P(None, "tp", "fsdp"),
        P("tp", "fsdp"),
        P("fsdp"),
        P("fsdp"),
        P("fsdp"),
        P("fsdp", "tp"),
        P("tp", "fsdp"),
        P("tp", "fsdp"),
        P("fsdp"),
        P("fsdp", ("ctx", "tp"), None),
    )
    return jax.shard_map(
        local,
        mesh=mesh,
        in_specs=placed,
        out_specs=(
            P("fsdp", ("ctx", "tp"), None),
            P("fsdp", ("ctx", "tp"), None),
            P("fsdp"),
            P("fsdp"),
            P(None, "fsdp", "tp"),
            P(None, "tp", "fsdp"),
            P("tp", "fsdp"),
            P("fsdp"),
            P("fsdp"),
            P("fsdp"),
            P("fsdp", "tp"),
            P("tp", "fsdp"),
            P("tp", "fsdp"),
            P("fsdp"),
        ),
        check_vma=False,
    )
```

```python
from functools import partial

import jax
import jax.numpy as jnp
from jax import lax
from jax.experimental import pallas as pl
from jax.experimental.pallas import tpu as pltpu
from jax.sharding import PartitionSpec as P

EPSILON = 1e-05
MASKED = -1e30
F32 = jnp.float32
BF16 = jnp.bfloat16
HEAD = 64
PAIR = 2 * HEAD


def norm_rows(values, gain, shift):
    average = jnp.mean(values, axis=-1, keepdims=True)
    centred = values - average
    spread = jnp.mean(centred * centred, axis=-1, keepdims=True)
    return centred * lax.rsqrt(spread + EPSILON) * gain + shift


def norm_back(values, gain, upstream):
    average = jnp.mean(values, axis=-1, keepdims=True)
    centred = values - average
    spread = jnp.mean(centred * centred, axis=-1, keepdims=True)
    inverse = lax.rsqrt(spread + EPSILON)
    unit = centred * inverse
    scaled = upstream * gain
    inner = jnp.mean(scaled * unit, axis=-1, keepdims=True)
    grad = (scaled - jnp.mean(scaled, axis=-1, keepdims=True) - unit * inner) * inverse
    return grad, jnp.sum(upstream * unit, axis=(0, 1)), jnp.sum(upstream, axis=(0, 1))


def swap(values, axis):
    return lax.ppermute(values, axis, [(0, 1), (1, 0)])


def dot(left, right, dims):
    return lax.dot_general(left, right, (dims, ((), ())), preferred_element_type=F32)


def head_parts(matrix):
    lane = lax.broadcasted_iota(jnp.int32, matrix.shape, 1)
    zero = jnp.zeros_like(matrix)
    return jnp.where(lane < HEAD, matrix, zero), jnp.where(lane < HEAD, zero, matrix)


def forward_kernel(
    chunk_count, q_segs, k_segs, q_ref, k_ref, v_ref, o_ref, lse_ref, peak, total, acc
):
    block = q_ref.shape[1]
    seq, qblk = pl.program_id(0), pl.program_id(2)
    q_seg = q_segs[seq, qblk]
    peak[...] = jnp.full(peak.shape, MASKED, F32)
    total[...] = jnp.zeros(total.shape, F32)
    acc[...] = jnp.zeros(acc.shape, F32)
    q_parts = head_parts(q_ref[0] * jnp.asarray(HEAD**-0.5, BF16))

    def chunk(index, diagonal):
        rows = pl.ds(index * block, block)
        keys = k_ref[0, rows, :]
        v_parts = head_parts(v_ref[0, rows, :])
        scales, terms = [], []
        for head in range(2):
            scores = dot(q_parts[head], keys, ((1,), (1,)))
            if diagonal:
                q_at = lax.broadcasted_iota(jnp.int32, scores.shape, 0)
                k_at = lax.broadcasted_iota(jnp.int32, scores.shape, 1)
                scores = jnp.where(k_at <= q_at, scores, MASKED)
            old = peak[head]
            new = jnp.maximum(old, jnp.max(scores, axis=1, keepdims=True))
            probs = jnp.exp(scores - new[:, :1])
            scale = jnp.exp(old - new)
            total[head] = total[head] * scale + jnp.sum(probs, axis=1, keepdims=True)
            peak[head] = new
            scales.append(scale)
            terms.append(dot(probs.astype(BF16), v_parts[head], ((1,), (0,))))
        lane = lax.broadcasted_iota(jnp.int32, acc.shape, 1)
        acc[...] = acc[...] * jnp.where(lane < HEAD, scales[0], scales[1]) + (terms[0] + terms[1])

    for index in range(chunk_count):
        k_seg = k_segs[seq, index]
        pl.when(k_seg == q_seg)(partial(chunk, index, True))
        pl.when(k_seg < q_seg)(partial(chunk, index, False))
    lane = lax.broadcasted_iota(jnp.int32, acc.shape, 1)
    sums = jnp.where(lane < HEAD, total[0], total[1])
    o_ref[0] = (acc[...] / sums).astype(BF16)
    lse = jnp.transpose(jnp.where(lane < HEAD, peak[0], peak[1]) + jnp.log(sums))
    lse_ref[0, 0] = jnp.concatenate([lse[0:4], lse[HEAD : HEAD + 4]], axis=0)


def backward_kernel(
    chunk_count,
    q_segs,
    k_segs,
    q_ref,
    g_ref,
    o_ref,
    lse_ref,
    k_ref,
    v_ref,
    dq_ref,
    dkv_ref,
    dq_acc,
    dk_acc,
    dv_acc,
):
    block = q_ref.shape[1]
    seq, qblk = pl.program_id(0), pl.program_id(2)
    q_seg = q_segs[seq, qblk]

    @pl.when(qblk == 0)
    def _():
        dk_acc[...] = jnp.zeros(dk_acc.shape, F32)
        dv_acc[...] = jnp.zeros(dv_acc.shape, F32)

    dq_acc[...] = jnp.zeros(dq_acc.shape, F32)
    q_parts = head_parts(q_ref[0] * jnp.asarray(HEAD**-0.5, BF16))
    g_parts = head_parts(g_ref[0])
    products = jnp.transpose(g_ref[0].astype(F32) * o_ref[0].astype(F32))
    deltas = (
        jnp.sum(products[:HEAD], axis=0, keepdims=True),
        jnp.sum(products[HEAD:], axis=0, keepdims=True),
    )
    lses = (lse_ref[0, 0, 0:1, :], lse_ref[0, 0, 4:5, :])

    def chunk(index, diagonal):
        rows = pl.ds(index * block, block)
        keys = k_ref[0, rows, :]
        values = v_ref[0, rows, :]
        k_parts = head_parts(keys)
        dk, dv, dq = dk_acc[rows, :], dv_acc[rows, :], dq_acc[...]
        for head in range(2):
            scores = dot(keys, q_parts[head], ((1,), (1,)))
            if diagonal:
                k_at = lax.broadcasted_iota(jnp.int32, scores.shape, 0)
                q_at = lax.broadcasted_iota(jnp.int32, scores.shape, 1)
                scores = jnp.where(k_at <= q_at, scores, MASKED)
            probs = jnp.exp(scores - lses[head])
            up = dot(values, g_parts[head], ((1,), (1,)))
            scaled = (probs * (up - deltas[head])).astype(BF16)
            dv = dv + dot(probs.astype(BF16), g_parts[head], ((1,), (0,)))
            dk = dk + dot(scaled, q_parts[head], ((1,), (0,)))
            dq = dq + dot(scaled, k_parts[head], ((0,), (0,)))
        dk_acc[rows, :] = dk
        dv_acc[rows, :] = dv
        dq_acc[...] = dq

    for index in range(chunk_count):
        k_seg = k_segs[seq, index]
        pl.when(k_seg == q_seg)(partial(chunk, index, True))
        pl.when(k_seg < q_seg)(partial(chunk, index, False))
    dq_ref[0] = (dq_acc[...] * HEAD**-0.5).astype(BF16)

    @pl.when(qblk == pl.num_programs(2) - 1)
    def _():
        dkv_ref[0, 0] = dk_acc[...].astype(BF16)
        dkv_ref[0, 1] = dv_acc[...].astype(BF16)


def attend(queries, kv_all, q_segs, k_segs, block):
    seqs, rows, width = queries.shape
    total_len = kv_all.shape[1]
    pairs = width // PAIR
    q_spec = pl.BlockSpec((1, block, PAIR), lambda s, p, q, *_: (s, q, p))
    return pl.pallas_call(
        partial(forward_kernel, total_len // block),
        grid_spec=pltpu.PrefetchScalarGridSpec(
            num_scalar_prefetch=2,
            grid=(seqs, pairs, rows // block),
            in_specs=[
                q_spec,
                pl.BlockSpec((1, total_len, PAIR), lambda s, p, q, *_: (s, 0, p)),
                pl.BlockSpec((1, total_len, PAIR), lambda s, p, q, *_: (s, 0, p + pairs)),
            ],
            out_specs=[
                q_spec,
                pl.BlockSpec((1, 1, 8, block), lambda s, p, q, *_: (s, p, 0, q)),
            ],
            scratch_shapes=[
                pltpu.VMEM((2, block, PAIR), F32),
                pltpu.VMEM((2, block, PAIR), F32),
                pltpu.VMEM((block, PAIR), F32),
            ],
        ),
        out_shape=[
            jax.ShapeDtypeStruct(queries.shape, BF16),
            jax.ShapeDtypeStruct((seqs, pairs, 8, rows), F32),
        ],
        compiler_params=pltpu.CompilerParams(vmem_limit_bytes=40 * 2**20),
        cost_estimate=pl.CostEstimate(
            flops=16 * seqs * rows * total_len * width,
            bytes_accessed=8 * seqs * total_len * width,
            transcendentals=seqs * rows * total_len * width // HEAD,
        ),
    )(q_segs, k_segs, queries, kv_all, kv_all)


def attend_back(queries, grads, mixed, lse, kv_all, q_segs, k_segs, block):
    seqs, rows, width = queries.shape
    total_len = kv_all.shape[1]
    pairs = width // PAIR
    q_spec = pl.BlockSpec((1, block, PAIR), lambda s, p, q, *_: (s, q, p))
    return pl.pallas_call(
        partial(backward_kernel, total_len // block),
        grid_spec=pltpu.PrefetchScalarGridSpec(
            num_scalar_prefetch=2,
            grid=(seqs, pairs, rows // block),
            in_specs=[
                q_spec,
                q_spec,
                q_spec,
                pl.BlockSpec((1, 1, 8, block), lambda s, p, q, *_: (s, p, 0, q)),
                pl.BlockSpec((1, total_len, PAIR), lambda s, p, q, *_: (s, 0, p)),
                pl.BlockSpec((1, total_len, PAIR), lambda s, p, q, *_: (s, 0, p + pairs)),
            ],
            out_specs=[
                q_spec,
                pl.BlockSpec((1, 2, total_len, PAIR), lambda s, p, q, *_: (s, 0, 0, p)),
            ],
            scratch_shapes=[
                pltpu.VMEM((block, PAIR), F32),
                pltpu.VMEM((total_len, PAIR), F32),
                pltpu.VMEM((total_len, PAIR), F32),
            ],
        ),
        out_shape=[
            jax.ShapeDtypeStruct(queries.shape, BF16),
            jax.ShapeDtypeStruct((seqs, 2, total_len, width), BF16),
        ],
        compiler_params=pltpu.CompilerParams(vmem_limit_bytes=48 * 2**20),
        cost_estimate=pl.CostEstimate(
            flops=40 * seqs * rows * total_len * width,
            bytes_accessed=16 * seqs * total_len * width,
            transcendentals=seqs * rows * total_len * width // HEAD,
        ),
    )(q_segs, k_segs, queries, grads, mixed, lse, kv_all, kv_all)


def pair_rows(values):
    return jnp.concatenate([values, swap(values, "tp")], axis=1)


def pair_sum(terms, half_rows):
    terms = terms.reshape(-1, 2 * half_rows, terms.shape[-1])
    other = swap(terms[:, half_rows:].astype(BF16), "tp")
    return terms[:, :half_rows].astype(BF16).astype(F32) + other.astype(F32)


def axis_bits():
    return (lax.axis_size("fsdp") - 1).bit_length()


def halving_orders():
    bits = axis_bits()
    highest = list(range(bits - 1, 0, -1))
    if lax.axis_size("ctx") == 2:
        return (
            ["ctx", 0] + highest,
            [0] + highest[:1] + ["ctx"] + highest[1:],
        )
    return [0] + highest, highest[:1] + [0] + highest[1:]


def flip(values, bit):
    if bit == "ctx":
        return swap(values, "ctx")
    count = lax.axis_size("fsdp")
    return lax.ppermute(values, "fsdp", [(i, i ^ (1 << bit)) for i in range(count)])


def own_bit(bit):
    if bit == "ctx":
        return lax.axis_index("ctx")
    return (lax.axis_index("fsdp") >> bit) & 1


def scatter_sum(values, order):
    shards, rows, columns = values.shape
    bits = axis_bits()
    left = list(range(bits - 1, -1, -1))
    if "ctx" in order:
        left.append("ctx")
        rows //= 2
    values = values.reshape((2,) * len(left) + (rows, columns))
    for bit in order:
        at, mine = left.index(bit), own_bit(bit)
        sent = lax.dynamic_index_in_dim(values, 1 - mine, at, keepdims=False)
        kept = lax.dynamic_index_in_dim(values, mine, at, keepdims=False)
        values = kept.astype(F32) + flip(sent, bit).astype(F32)
        if len(left) > 1:
            values = values.astype(sent.dtype)
        left.remove(bit)
    if "ctx" not in order:
        if lax.axis_size("ctx") == 2:
            return values + swap(values, "ctx")
        return lax.psum(values.astype(BF16), "ctx").astype(F32)
    values = values.astype(BF16)
    other = swap(values, "ctx")
    first = lax.axis_index("ctx") == 0
    low, high = jnp.where(first, values, other), jnp.where(first, other, values)
    return jnp.concatenate([low, high], axis=0).astype(F32)


def gather(values, order):
    rows, columns = values.shape
    held = []
    if "ctx" in order:
        halves = values.reshape(2, rows // 2, columns)
        values = lax.dynamic_index_in_dim(halves, own_bit("ctx"), 0, keepdims=False)
    for bit in reversed(order):
        rank = -1 if bit == "ctx" else bit
        at = sum(1 for one in held if one > rank)
        held.append(rank)
        other = flip(values, bit)
        first = own_bit(bit) == 0
        low, high = jnp.where(first, values, other), jnp.where(first, other, values)
        values = jnp.stack([low, high], axis=at)
    return values.reshape(-1, rows, columns)


def local(
    tokens,
    segment_order,
    ln1_gain,
    ln1_bias,
    qkv_weight,
    qv_bias,
    out_weight,
    out_bias,
    ln2_gain,
    ln2_bias,
    up_weight,
    up_bias,
    down_weight,
    down_bias,
    cotangent,
):
    shards = lax.axis_size("fsdp")
    contexts = lax.axis_size("ctx")
    seq_count, half_rows, model_width = tokens.shape
    local_rows = half_rows * 2
    depth = model_width // shards
    inner_width = qkv_weight.shape[2]
    heads = qv_bias.shape[1]
    hidden = up_weight.shape[1]
    units = up_bias.shape[0]
    qkv_width = 3 * inner_width

    smalls = [ln1_gain, ln1_bias, out_bias, ln2_gain, ln2_bias, down_bias]
    flat = jnp.concatenate([part.reshape(-1) for part in smalls + [qv_bias, up_bias]])
    flat = jnp.pad(flat, (0, qkv_width - flat.shape[0])).reshape(1, qkv_width)
    flat = jnp.pad(flat, ((0, 15), (0, 0)))
    order_a, order_b = halving_orders()
    cut = -(-qkv_width // 256) * 128
    first = jnp.concatenate(
        [jnp.swapaxes(qkv_weight, 0, 1).reshape(depth, qkv_width), flat], axis=0
    )
    first_all = jnp.concatenate(
        [gather(first[:, :cut], order_a), gather(first[:, cut:], order_b)], axis=2
    )
    qkv_full = first_all[:, :depth].reshape(model_width, qkv_width)
    small_all = first_all[:, depth].astype(F32)
    gain_one, shift_one, outb_full, gain_two, shift_two, downb_full = [
        small_all[:, i * depth : (i + 1) * depth].reshape(model_width) for i in range(6)
    ]
    start = 6 * depth
    span = qv_bias.shape[2]
    qv_size = 2 * heads * span
    qv_full = jnp.moveaxis(
        small_all[:, start : start + qv_size].reshape(shards, 2, heads, span), 0, 2
    ).reshape(2, inner_width)
    start += qv_size
    upb_full = jnp.moveaxis(
        small_all[:, start : start + units * span].reshape(shards, units, span), 0, 1
    ).reshape(hidden)

    residual_in = tokens.astype(F32)
    normed_one = norm_rows(residual_in, gain_one, shift_one).astype(BF16)
    rows_one = pair_rows(normed_one)
    grad_flat = pair_rows(cotangent).reshape(-1, model_width)
    flat_one = rows_one.reshape(-1, model_width)
    kv = jnp.dot(flat_one, qkv_full[:, inner_width:], preferred_element_type=F32)
    kv_bias = jnp.concatenate([jnp.zeros((inner_width,), F32), qv_full[1]])
    kv = (kv + kv_bias).astype(BF16).reshape(seq_count, local_rows, 2 * inner_width)
    queries = jnp.dot(flat_one, qkv_full[:, :inner_width], preferred_element_type=F32)
    queries = (queries + qv_full[0]).astype(BF16).reshape(seq_count, local_rows, inner_width)

    out_up = jnp.concatenate([up_weight, out_weight.T], axis=1)
    normed_one, out_up, down_own = lax.optimization_barrier((normed_one, out_up, down_weight.T))
    wide_all = gather(out_up, order_b).reshape(model_width, hidden + inner_width)
    up_full, out_t = wide_all[:, :hidden], wide_all[:, hidden:]
    down_t = gather(down_own, order_a).reshape(model_width, hidden)

    here, core = lax.axis_index("ctx"), lax.axis_index("tp")
    if contexts == 2:
        kv_all = jnp.concatenate([kv, swap(kv, "ctx")], axis=1)
        order = [here, 1 - here]
    else:
        kv_all = lax.all_gather(kv, "ctx", axis=1, tiled=True)
        order = list(range(contexts))
    segment_size = contexts * local_rows // segment_order.shape[1]
    block = min(segment_size, half_rows)
    per_half = half_rows // segment_size

    def half_segments(context):
        picks = []
        for turn in range(2):
            at = (context * 2 + (core + turn) % 2) * per_half
            picks.append(lax.dynamic_slice_in_dim(segment_order, at, per_half, 1))
        return jnp.concatenate(picks, axis=1)

    q_segs = half_segments(here)
    k_segs = jnp.concatenate([half_segments(context) for context in order], axis=1)
    mixed, lse = attend(queries, kv_all, q_segs, k_segs, block)
    mixed_flat = mixed.reshape(-1, inner_width)

    attn_part = pair_sum(dot(mixed_flat, out_t, ((1,), (1,))), half_rows)
    resid_mid = residual_in + attn_part + outb_full
    normed_two = norm_rows(resid_mid, gain_two, shift_two).astype(BF16)
    flat_two = pair_rows(normed_two).reshape(-1, model_width)
    pre_act = jnp.dot(flat_two, up_full, preferred_element_type=F32) + upb_full
    activated, gelu_pull = jax.vjp(partial(jax.nn.gelu, approximate=True), pre_act)
    activated = activated.astype(BF16)
    act_grad = jnp.dot(grad_flat, down_t, preferred_element_type=F32)
    pre_grad = gelu_pull(act_grad)[0].astype(BF16)
    norm_two_grad = pair_sum(dot(pre_grad, up_full, ((1,), (1,))), half_rows)
    upstream = cotangent.astype(F32)
    mid_grad, gain_two_grad, shift_two_grad = norm_back(resid_mid, gain_two, norm_two_grad)
    resid_grad = upstream + mid_grad
    branch_flat = pair_rows(resid_grad.astype(BF16)).reshape(-1, model_width)
    mixed_grad = jnp.dot(branch_flat, out_t, preferred_element_type=F32).astype(BF16)
    up_grad = dot(flat_two, pre_grad, ((0,), (0,))).astype(BF16)
    down_grad = dot(grad_flat, activated, ((0,), (0,))).astype(BF16)
    out_grad = dot(branch_flat, mixed_flat, ((0,), (0,))).astype(BF16)
    wide = jnp.concatenate([up_grad, out_grad], axis=1)
    wide, down_grad, mixed_grad = lax.optimization_barrier((wide, down_grad, mixed_grad))
    down_total = scatter_sum(down_grad.reshape(shards, depth, hidden), order_a)
    wide_total = scatter_sum(wide.reshape(shards, depth, hidden + inner_width), order_b)

    query_grad, kv_grad = attend_back(
        queries,
        mixed_grad.reshape(queries.shape),
        mixed,
        lse,
        kv_all,
        q_segs,
        k_segs,
        block,
    )
    if contexts == 2:
        kv_own = kv_grad[:, :, :local_rows].astype(F32)
        kv_own = kv_own + swap(kv_grad[:, :, local_rows:], "ctx").astype(F32)
        kv_own = kv_own.astype(BF16)
    else:
        kv_own = lax.psum_scatter(kv_grad, "ctx", scatter_dimension=2, tiled=True)
    stacked = jnp.concatenate([query_grad, kv_own[:, 0], kv_own[:, 1]], axis=2)
    stacked = stacked.reshape(-1, qkv_width)
    norm_one_grad = pair_sum(dot(stacked, qkv_full, ((1,), (1,))), half_rows)
    qkv_grad = dot(flat_one, stacked, ((0,), (0,))).astype(BF16)
    qkv_grad = qkv_grad.reshape(shards, depth, qkv_width)
    qkv_total = jnp.concatenate(
        [
            scatter_sum(qkv_grad[:, :, :cut], order_a),
            scatter_sum(qkv_grad[:, :, cut:], order_b),
        ],
        axis=1,
    )

    mlp_terms = dot(activated, down_t, ((1,), (1,)))
    mlp_part = pair_sum(mlp_terms, half_rows)
    output = (resid_mid + mlp_part + downb_full).astype(BF16)

    input_part, gain_one_grad, shift_one_grad = norm_back(residual_in, gain_one, norm_one_grad)
    tokens_grad = (resid_grad + input_part).astype(BF16)
    norm_grads = jnp.stack(
        [
            gain_one_grad,
            shift_one_grad,
            jnp.sum(resid_grad, axis=(0, 1)),
            gain_two_grad,
            shift_two_grad,
            jnp.sum(upstream, axis=(0, 1)),
        ]
    )
    norm_grads = norm_grads + swap(norm_grads, "tp")
    bias_sums = jnp.sum(stacked.astype(F32), axis=0)
    qv_grad = jnp.stack([bias_sums[:inner_width], bias_sums[2 * inner_width :]])
    upb_grad = jnp.sum(pre_grad.astype(F32), axis=0)
    small_rows = jnp.concatenate(
        [
            jnp.swapaxes(norm_grads.reshape(6, shards, depth), 0, 1).reshape(shards, -1),
            jnp.moveaxis(qv_grad.reshape(2, heads, shards, span), 2, 0).reshape(shards, -1),
            jnp.moveaxis(upb_grad.reshape(units, shards, span), 1, 0).reshape(shards, -1),
        ],
        axis=1,
    )
    small_size = -(-small_rows.shape[1] // 1024) * 1024
    small_rows = jnp.pad(small_rows, ((0, 0), (0, small_size - small_rows.shape[1])))
    small = small_rows.reshape(shards, small_size // 128, 128)
    plain = [bit for bit in order_a if bit != "ctx"]
    small = scatter_sum(small, plain).reshape(small_size)
    start = 6 * depth
    return (
        output,
        tokens_grad,
        small[:depth],
        small[depth : 2 * depth],
        jnp.swapaxes(qkv_total.reshape(depth, 3, inner_width), 0, 1),
        small[start : start + qv_size].reshape(2, heads, span),
        wide_total[:, hidden:].T,
        small[2 * depth : 3 * depth],
        small[3 * depth : 4 * depth],
        small[4 * depth : 5 * depth],
        wide_total[:, :hidden],
        small[start + qv_size : start + qv_size + units * span].reshape(units, span),
        down_total.T,
        small[5 * depth : 6 * depth],
    )


def solution(mesh):
    placed = (
        P("fsdp", ("ctx", "tp"), None),
        P("fsdp", None),
        P("fsdp"),
        P("fsdp"),
        P(None, "fsdp", "tp"),
        P(None, "tp", "fsdp"),
        P("tp", "fsdp"),
        P("fsdp"),
        P("fsdp"),
        P("fsdp"),
        P("fsdp", "tp"),
        P("tp", "fsdp"),
        P("tp", "fsdp"),
        P("fsdp"),
        P("fsdp", ("ctx", "tp"), None),
    )
    return jax.shard_map(
        local,
        mesh=mesh,
        in_specs=placed,
        out_specs=(
            P("fsdp", ("ctx", "tp"), None),
            P("fsdp", ("ctx", "tp"), None),
            P("fsdp"),
            P("fsdp"),
            P(None, "fsdp", "tp"),
            P(None, "tp", "fsdp"),
            P("tp", "fsdp"),
            P("fsdp"),
            P("fsdp"),
            P("fsdp"),
            P("fsdp", "tp"),
            P("tp", "fsdp"),
            P("tp", "fsdp"),
            P("fsdp"),
        ),
        check_vma=False,
    )
```
